256 devices in a mesh: rows: 32 (over z, x), rhs: 8 (over y, core).
Axes of the slice: x: 4, y: 4, z: 8, core: 2. Of those that a mesh axis runs over, the one named last changes fastest.
Arguments:
- right_side: float32 [32768, 1024], P('rows', 'rhs'), may hold values from -6 to 6
- leaf_blocks: bfloat16 [128, 2, 256, 256], P('rows'), may hold values from -0.25 to 0.25
- out_basis: bfloat16 [128, 2, 256, 128], P('rows'), may hold values from -0.375 to 0.375
- in_basis: bfloat16 [128, 2, 256, 128], P('rows'), may hold values from -0.25 to 0.25
- couplings: bfloat16 [128, 7, 2, 128, 128], P('rows'), may hold values from -6 to 6
Outputs:
- solution: float32 [2, 32768, 1024], P(None, 'rows', 'rhs')
The draws below stay inside these ranges and needn't reach their ends.
All inputs are finite; a program needn't handle non-finite values.
Results may differ from the reference program's by a relative error of at most 0.0043.
Values sent between devices are 32-bit elements; how exact they have to be, the bound alone decides.
No kernel may reach another device: no remote copies, remote signals or barrier semaphores. Data moves between devices by JAX's collectives and lax.ppermute only.
A program may use at most 64 MiB of HBM per device.

```python
import math
import jax
import jax.numpy as jnp
from jax import lax

LEAF = 256
RANK = 128
RHS_DEV = 128
ROWS_DEV = 1024
ORDER = 32768
RHS = 1024
LEAVES = 128
LEVELS = 7
N_ROWS = 32
N_RHS = 8


def shard_levels(own_key, dims, pieces, smallest, largest):
    factor_of = 1.0
    for position, blocks in pieces:
        draws = jax.random.uniform(jax.random.fold_in(jax.random.fold_in(own_key, 6), position), (blocks,), jnp.float32, smallest / len(pieces), largest / len(pieces))
        factor_of = factor_of * jnp.repeat(jnp.exp(draws), dims[position] // blocks).reshape((-1,) + (1,) * (len(dims) - 1 - position))
    return factor_of


def bell_draw(rng, shape, scale, reach, pieces=(), held_as=jnp.bfloat16):
    array = scale * jax.random.normal(rng, shape, jnp.float32)
    if pieces:
        array = array * shard_levels(rng, shape, pieces, -0.22, 0.18)
    return jnp.clip(array, -reach, reach).astype(held_as)


def setup_inputs(seed: int = 0) -> dict:
    keys = jax.random.split(jax.random.key(seed), 6)
    right_side = bell_draw(keys[0], (ORDER, RHS), 1.0, 6.0, ((0, 32), (1, 8)), jnp.float32)
    leaf_blocks = bell_draw(keys[1], (LEAVES, 2, LEAF, LEAF), (2 * LEAF) ** -0.5, 0.25, ((0, 32),))
    out_basis = bell_draw(keys[2], (LEAVES, 2, LEAF, RANK), (2 * RANK) ** -0.5, 0.375, ((0, 32),))
    in_basis = bell_draw(keys[3], (LEAVES, 2, LEAF, RANK), (2 * LEAF) ** -0.5, 0.25, ((0, 32),))
    couplings = bell_draw(keys[4], (LEAVES, LEVELS, 2, RANK, RANK), 1.0, 6.0, ((0, 32),))
    return dict(right_side=right_side, leaf_blocks=leaf_blocks, out_basis=out_basis, in_basis=in_basis, couplings=couplings)


def rounded(values):
    return lax.optimization_barrier(values.astype(jnp.bfloat16)).astype(jnp.float32)

def complex_mix(pattern, left_re, left_im, right_re, right_im):
    highest = lax.Precision.HIGHEST
    real_part = jnp.einsum(pattern, left_re, right_re, precision=highest) - jnp.einsum(pattern, left_im, right_im, precision=highest)
    imag_part = jnp.einsum(pattern, left_re, right_im, precision=highest) + jnp.einsum(pattern, left_im, right_re, precision=highest)
    return (real_part, imag_part)

def sibling_sum(values, group):
    count, rank_size, columns = values.shape
    grouped = values.reshape(count // (2 * group), 2, group, rank_size, columns).sum(axis=2)
    swapped = grouped[:, ::-1]
    spread = jnp.broadcast_to(swapped[:, :, None], (count // (2 * group), 2, group, rank_size, columns))
    return spread.reshape(count, rank_size, columns)

def solve_columns(block, leaf_blocks, out_basis, in_basis, couplings):
    columns = block.shape[1]
    band_size = ROWS_DEV // N_ROWS
    spread = block.reshape(N_ROWS, ROWS_DEV, columns).transpose(1, 0, 2).reshape(ORDER, columns)
    spectrum = jnp.fft.fft(spread, axis=0) / math.sqrt(ORDER)
    spectrum = spectrum.reshape(N_ROWS, N_ROWS, band_size, columns).transpose(1, 0, 2, 3).reshape(LEAVES, LEAF, columns)
    leaves_re = rounded(jnp.real(spectrum).astype(jnp.float32))
    leaves_im = rounded(jnp.imag(spectrum).astype(jnp.float32))
    basis_in = in_basis.astype(jnp.float32)
    coeff_re, coeff_im = complex_mix('lar,lac->lrc', basis_in[:, 0], -basis_in[:, 1], leaves_re, leaves_im)
    field_re = jnp.zeros((LEAVES, RANK, columns), jnp.float32)
    field_im = jnp.zeros((LEAVES, RANK, columns), jnp.float32)
    for level_index in range(LEVELS):
        group = 2 ** level_index
        weight = (2.0 * RANK * LEVELS * group) ** (-0.5)
        near_re = rounded(weight * sibling_sum(coeff_re, group))
        near_im = rounded(weight * sibling_sum(coeff_im, group))
        coupling = couplings[:, level_index].astype(jnp.float32)
        part_re, part_im = complex_mix('lrs,lsc->lrc', coupling[:, 0], coupling[:, 1], near_re, near_im)
        field_re = field_re + part_re
        field_im = field_im + part_im
    field_re = rounded(field_re)
    field_im = rounded(field_im)
    diagonal = leaf_blocks.astype(jnp.float32)
    basis_out = out_basis.astype(jnp.float32)
    own_re, own_im = complex_mix('lab,lbc->lac', diagonal[:, 0], diagonal[:, 1], leaves_re, leaves_im)
    far_re, far_im = complex_mix('lar,lrc->lac', basis_out[:, 0], basis_out[:, 1], field_re, field_im)
    image = lax.complex(own_re + far_re, own_im + far_im)
    image = image.reshape(N_ROWS, N_ROWS, band_size, columns).transpose(1, 0, 2, 3).reshape(ORDER, columns)
    values = jnp.fft.ifft(image, axis=0) * math.sqrt(ORDER)
    values = values.reshape(ROWS_DEV, N_ROWS, columns).transpose(1, 0, 2).reshape(ORDER, columns)
    return jnp.stack([jnp.real(values), jnp.imag(values)]).astype(jnp.float32)

def reference(right_side, leaf_blocks, out_basis, in_basis, couplings):
    blocks = right_side.reshape(ORDER, N_RHS, RHS_DEV).transpose(1, 0, 2)

    def one_block(block):
        return solve_columns(block, leaf_blocks, out_basis, in_basis, couplings)
    solved = lax.map(one_block, blocks)
    return solved.transpose(1, 2, 0, 3).reshape(2, ORDER, RHS)
```

```python
import math

import jax
import jax.numpy as jnp
import ml_dtypes
import numpy as np
from jax import lax
from jax.experimental import pallas as pl
from jax.experimental.pallas import tpu as pltpu
from jax.sharding import PartitionSpec as P

HALF = 128
LANES = 2 * HALF
ROWS = 32
BAND = 32
LENGTH = ROWS * BAND
ORDER = LENGTH * ROWS
NORM = 1.0 / math.sqrt(ORDER)
LEAF = 256
RANK = 128
LEVELS = 7
LEAVES = 4
INNER = 2
UPPER = 5
RADIX = 8
POINTS = LENGTH // RADIX


def split_table(table):
    high = table.astype(ml_dtypes.bfloat16)
    low = (table - high.astype(np.float64)).astype(ml_dtypes.bfloat16)
    return high, low


def forward_tables():
    b = np.arange(RADIX)[:, None, None]
    k = np.arange(POINTS)[None, :, None]
    a = np.arange(POINTS)[None, None, :]
    angle = -2.0 * np.pi * (((8 * a + b) * k) % LENGTH) / LENGTH
    high, low = split_table(np.concatenate([np.cos(angle), np.sin(angle)], 1))
    return np.concatenate([high, low, high], 2)


def inverse_tables():
    b = np.arange(RADIX)[:, None, None]
    a = np.arange(POINTS)[None, :, None]
    k = np.arange(POINTS)[None, None, :]
    angle = 2.0 * np.pi * (((8 * a + b) * k) % LENGTH) / LENGTH
    high, low = split_table(NORM * np.concatenate([np.cos(angle), np.sin(angle)], 2))
    return np.concatenate([high, low, high], 2)


def times_i(x):
    return jnp.concatenate([-x[:, HALF:], x[:, :HALF]], 1)


def packed_fft(values, sign):
    count = len(values)
    if count == 1:
        return values
    even = packed_fft(values[0::2], sign)
    odd = packed_fft(values[1::2], sign)
    half = count // 2
    out = [None] * count
    for k in range(half):
        x = odd[k]
        if k == 0:
            t = x
        elif 4 * k == count:
            t = times_i(x)
            if sign < 0:
                t = -t
        else:
            angle = sign * 2.0 * math.pi * k / count
            t = math.cos(angle) * x + math.sin(angle) * times_i(x)
        out[k] = even[k] + t
        out[k + half] = even[k] - t
    return out


def split_fft(values, sign):
    count = len(values)
    if count == 1:
        return values
    even = split_fft(values[0::2], sign)
    odd = split_fft(values[1::2], sign)
    half = count // 2
    out = [None] * count
    for k in range(half):
        re, im = odd[k]
        if k == 0:
            t = (re, im)
        elif 4 * k == count:
            t = (-im, re) if sign > 0 else (im, -re)
        else:
            c = math.cos(2.0 * math.pi * k / count)
            s = sign * math.sin(2.0 * math.pi * k / count)
            t = (c * re - s * im, c * im + s * re)
        e = even[k]
        out[k] = (e[0] + t[0], e[1] + t[1])
        out[k + half] = (e[0] - t[0], e[1] - t[1])
    return out


def small_phase(x):
    y = x * x
    c = 1.0 + y * (-1.0 / 2 + y * (1.0 / 24 + y * (-1.0 / 720 + y * (1.0 / 40320 - y / 3628800.0))))
    s = x * (1.0 + y * (-1.0 / 6 + y * (1.0 / 120 + y * (-1.0 / 5040 + y * (1.0 / 362880 - y / 39916800.0)))))
    return c, s


def cmul(x, y):
    return (x[0] * y[0] - x[1] * y[1], x[0] * y[1] + x[1] * y[0])


def block_phases(device, sign):
    shape = (8, HALF)
    step = jnp.full(shape, 1.0, jnp.float32) * (device.astype(jnp.float32) * (sign * 2.0 * math.pi / 256.0))
    one = small_phase(step)
    two = cmul(one, one)
    four = cmul(two, two)
    three = cmul(two, one)
    return [None, one, two, three, four, cmul(four, one), cmul(four, two), cmul(four, three)]


def row_phase(device, start, sign):
    row = (lax.broadcasted_iota(jnp.int32, (8, HALF), 0) + start).astype(jnp.float32)
    return small_phase(row * (device.astype(jnp.float32) * (sign * 2.0 * math.pi / ORDER)))


def forward_kernel(x_ref, table_ref, out_ref, part_ref):
    device = lax.axis_index("rows")
    for b in range(RADIX):
        x = x_ref[pl.ds(b, POINTS, stride=RADIX), :]
        high = x.astype(jnp.bfloat16)
        low = (x - high.astype(jnp.float32)).astype(jnp.bfloat16)
        part_ref[b] = jnp.dot(
            table_ref[b], jnp.concatenate([high, high, low], 0), preferred_element_type=jnp.float32
        )
    blocks = block_phases(device, -1.0)
    for g in range(POINTS // 8):
        rows = row_phase(device, 8 * g, -1.0)
        values = [
            (part_ref[b, 8 * g : 8 * g + 8, :], part_ref[b, POINTS + 8 * g : POINTS + 8 * g + 8, :])
            for b in range(RADIX)
        ]
        values = split_fft(values, -1)
        for k in range(RADIX):
            phase = rows if k == 0 else cmul(rows, blocks[k])
            re, im = cmul(values[k], phase)
            at = POINTS * k + 8 * g
            out_ref[at // BAND, at % BAND : at % BAND + 8, :HALF] = re
            out_ref[at // BAND, at % BAND : at % BAND + 8, HALF:] = im


def forward_call(x):
    shape = jax.ShapeDtypeStruct((ROWS, BAND, LANES), jnp.float32)
    table = jnp.asarray(forward_tables())
    vmem = pl.BlockSpec(memory_space=pltpu.VMEM)
    return pl.pallas_call(
        forward_kernel,
        out_shape=shape,
        in_specs=[vmem, vmem],
        out_specs=vmem,
        scratch_shapes=[pltpu.VMEM((RADIX, 2 * POINTS, HALF), jnp.float32)],
        compiler_params=pltpu.CompilerParams(vmem_limit_bytes=16 * 2**20),
        cost_estimate=pl.CostEstimate(flops=3 * 10**8, bytes_accessed=3 * 2**20, transcendentals=0),
        name="local_forward",
    )(x, table)


def transposed_dot(left, right):
    return lax.dot_general(left, right, (((0,), (0,)), ((), ())), preferred_element_type=jnp.float32)


def coefficient_kernel(block_ref, basis_ref, ordered_ref, coeff_ref, total_ref, scratch_ref):
    for g in range(BAND // 8):
        values = packed_fft([block_ref[d, 8 * g : 8 * g + 8, :] for d in range(ROWS)], -1)
        for j in range(ROWS):
            scratch_ref[BAND * j + 8 * g : BAND * j + 8 * g + 8, :] = NORM * values[j]
    total = None
    for leaf in range(LEAVES):
        x = scratch_ref[LEAF * leaf : LEAF * (leaf + 1), :]
        rounded = x.astype(jnp.bfloat16)
        turned = times_i(x).astype(jnp.bfloat16)
        ordered_ref[leaf, :LEAF, :] = rounded
        ordered_ref[leaf, LEAF:, :] = turned
        coeff = transposed_dot(basis_ref[leaf, 0], rounded) - transposed_dot(basis_ref[leaf, 1], turned)
        coeff_ref[leaf] = coeff
        total = coeff if total is None else total + coeff
    total_ref[...] = total


def coefficient_call(block, in_basis):
    vmem = pl.BlockSpec(memory_space=pltpu.VMEM)
    return pl.pallas_call(
        coefficient_kernel,
        out_shape=(
            jax.ShapeDtypeStruct((LEAVES, 2 * LEAF, LANES), jnp.bfloat16),
            jax.ShapeDtypeStruct((LEAVES, RANK, LANES), jnp.float32),
            jax.ShapeDtypeStruct((RANK, LANES), jnp.float32),
        ),
        in_specs=[vmem] * 2,
        out_specs=(vmem,) * 3,
        scratch_shapes=[pltpu.VMEM((LENGTH, LANES), jnp.float32)],
        compiler_params=pltpu.CompilerParams(vmem_limit_bytes=16 * 2**20),
        cost_estimate=pl.CostEstimate(flops=10**8, bytes_accessed=2 * 2**20, transcendentals=0),
        name="coefficients",
    )(block, in_basis)


def scale_of(level):
    return (2.0 * RANK * LEVELS * 2**level) ** (-0.5)


def with_turned(x):
    return [x.astype(jnp.bfloat16), times_i(x).astype(jnp.bfloat16)]


def near_kernel(ordered_ref, coeff_ref, blocks_ref, couplings_ref, own_ref, near_ref):
    for leaf in range(LEAVES):
        matrix = jnp.concatenate([blocks_ref[leaf, 0], blocks_ref[leaf, 1]], 1)
        own_ref[leaf] = jnp.dot(matrix, ordered_ref[leaf], preferred_element_type=jnp.float32)
        other = 2 * (1 - leaf // 2)
        siblings = with_turned(scale_of(0) * coeff_ref[leaf ^ 1]) + with_turned(
            scale_of(1) * (coeff_ref[other] + coeff_ref[other + 1])
        )
        matrix = jnp.concatenate([couplings_ref[leaf, t, part] for t in range(INNER) for part in range(2)], 1)
        near_ref[leaf] = jnp.dot(matrix, jnp.concatenate(siblings, 0), preferred_element_type=jnp.float32)


def near_call(ordered, coeff, leaf_blocks, couplings):
    vmem = pl.BlockSpec(memory_space=pltpu.VMEM)
    return pl.pallas_call(
        near_kernel,
        out_shape=(
            jax.ShapeDtypeStruct((LEAVES, LEAF, LANES), jnp.float32),
            jax.ShapeDtypeStruct((LEAVES, RANK, LANES), jnp.float32),
        ),
        in_specs=[vmem] * 4,
        out_specs=(vmem,) * 2,
        compiler_params=pltpu.CompilerParams(vmem_limit_bytes=16 * 2**20),
        cost_estimate=pl.CostEstimate(flops=2 * 10**8, bytes_accessed=4 * 2**20, transcendentals=0),
        name="near_field",
    )(ordered, coeff, leaf_blocks, couplings)


def image_kernel(own_ref, near_ref, couplings_ref, basis_ref, *refs):
    sibling_refs, out_ref, scratch_ref = refs[:UPPER], refs[UPPER], refs[UPPER + 1]
    siblings = []
    for level in range(UPPER):
        siblings += with_turned(scale_of(INNER + level) * sibling_refs[level][...])
    siblings = jnp.concatenate(siblings, 0)
    for leaf in range(LEAVES):
        matrix = jnp.concatenate(
            [couplings_ref[leaf, INNER + level, part] for level in range(UPPER) for part in range(2)], 1
        )
        field = near_ref[leaf] + jnp.dot(matrix, siblings, preferred_element_type=jnp.float32)
        matrix = jnp.concatenate([basis_ref[leaf, 0], basis_ref[leaf, 1]], 1)
        scratch_ref[LEAF * leaf : LEAF * (leaf + 1), :] = own_ref[leaf] + jnp.dot(
            matrix, jnp.concatenate(with_turned(field), 0), preferred_element_type=jnp.float32
        )
    for g in range(BAND // 8):
        values = packed_fft(
            [scratch_ref[BAND * j + 8 * g : BAND * j + 8 * g + 8, :] for j in range(ROWS)], 1
        )
        for d in range(ROWS):
            out_ref[d, 8 * g : 8 * g + 8, :] = values[d]


def image_call(own, near, couplings, out_basis, siblings):
    vmem = pl.BlockSpec(memory_space=pltpu.VMEM)
    return pl.pallas_call(
        image_kernel,
        out_shape=jax.ShapeDtypeStruct((ROWS, BAND, LANES), jnp.float32),
        in_specs=[vmem] * (4 + UPPER),
        out_specs=vmem,
        scratch_shapes=[pltpu.VMEM((LENGTH, LANES), jnp.float32)],
        compiler_params=pltpu.CompilerParams(vmem_limit_bytes=16 * 2**20),
        cost_estimate=pl.CostEstimate(flops=3 * 10**8, bytes_accessed=4 * 2**20, transcendentals=0),
        name="image",
    )(own, near, couplings, out_basis, *siblings)


def inverse_kernel(block_ref, table_ref, out_ref, turned_ref):
    device = lax.axis_index("rows")
    blocks = block_phases(device, 1.0)
    for g in range(POINTS // 8):
        rows = row_phase(device, 8 * g, 1.0)
        values = []
        for k in range(RADIX):
            phase = rows if k == 0 else cmul(rows, blocks[k])
            at = POINTS * k + 8 * g
            x = block_ref[at // BAND, at % BAND : at % BAND + 8, :]
            values.append(jnp.concatenate(cmul((x[:, :HALF], x[:, HALF:]), phase), 1))
        values = packed_fft(values, 1)
        for b in range(RADIX):
            turned_ref[b, 8 * g : 8 * g + 8, :] = values[b]
    for b in range(RADIX):
        x = turned_ref[b]
        high = x.astype(jnp.bfloat16)
        low = (x - high.astype(jnp.float32)).astype(jnp.bfloat16)
        high_y, low_y = times_i(high), times_i(low)
        value = jnp.dot(
            table_ref[b],
            jnp.concatenate([high, high_y, high, high_y, low, low_y], 0),
            preferred_element_type=jnp.float32,
        )
        out_ref[0, pl.ds(b, POINTS, stride=RADIX), :] = value[:, :HALF]
        out_ref[1, pl.ds(b, POINTS, stride=RADIX), :] = value[:, HALF:]


def inverse_call(block):
    vmem = pl.BlockSpec(memory_space=pltpu.VMEM)
    table = jnp.asarray(inverse_tables())
    return pl.pallas_call(
        inverse_kernel,
        out_shape=jax.ShapeDtypeStruct((2, LENGTH, HALF), jnp.float32),
        in_specs=[vmem] * 2,
        out_specs=vmem,
        scratch_shapes=[pltpu.VMEM((RADIX, POINTS, LANES), jnp.float32)],
        compiler_params=pltpu.CompilerParams(vmem_limit_bytes=16 * 2**20),
        cost_estimate=pl.CostEstimate(flops=3 * 10**8, bytes_accessed=3 * 2**20, transcendentals=0),
        name="local_inverse",
    )(block, table)


def exchange(total):
    held, siblings = total, []
    for bit in range(UPPER):
        pairs = [(i, i ^ (1 << bit)) for i in range(ROWS)]
        siblings.append(lax.ppermute(held, "rows", pairs))
        held = held + siblings[-1]
    return siblings


def swap_blocks(block):
    return lax.all_to_all(block, "rows", split_axis=0, concat_axis=0, tiled=True)


def shards(right_side, leaf_blocks, out_basis, in_basis, couplings):
    block = swap_blocks(forward_call(right_side))
    ordered, coeff, total = coefficient_call(block, in_basis)
    siblings = exchange(total)
    own, near = near_call(ordered, coeff, leaf_blocks, couplings)
    return inverse_call(swap_blocks(image_call(own, near, couplings, out_basis, siblings)))


def solution(mesh):
    placed = (
        P("rows", "rhs"),
        P("rows", None, None, None),
        P("rows", None, None, None),
        P("rows", None, None, None),
        P("rows", None, None, None, None),
    )
    return jax.shard_map(
        shards, mesh=mesh, in_specs=placed, out_specs=P(None, "rows", "rhs"), check_vma=False
    )
```

```python
import math

import jax
import jax.numpy as jnp
import ml_dtypes
import numpy as np
from jax import lax
from jax.experimental import pallas as pl
from jax.experimental.pallas import tpu as pltpu
from jax.sharding import PartitionSpec as P

HALF = 128
LANES = 2 * HALF
ROWS = 32
BAND = 32
LENGTH = ROWS * BAND
ORDER = LENGTH * ROWS
NORM = 1.0 / math.sqrt(ORDER)
LEAF = 256
RANK = 128
LEVELS = 7
LEAVES = 4
INNER = 2
UPPER = 5
EARLY = 4
RADIX = 8
POINTS = LENGTH // RADIX


def split_table(table):
    high = table.astype(ml_dtypes.bfloat16)
    low = (table - high.astype(np.float64)).astype(ml_dtypes.bfloat16)
    return high, low


def forward_table():
    k = np.arange(POINTS)[:, None]
    a = np.arange(POINTS)[None, :]
    angle = -2.0 * np.pi * ((a * k) % POINTS) / POINTS
    high, low = split_table(np.concatenate([np.cos(angle), np.sin(angle)], 0))
    return np.concatenate([high, low, high], 1)


def inverse_tables():
    b = np.arange(RADIX)[:, None, None]
    a = np.arange(POINTS)[None, :, None]
    k = np.arange(POINTS)[None, None, :]
    angle = 2.0 * np.pi * (((8 * a + b) * k) % LENGTH) / LENGTH
    high, low = split_table(NORM * np.concatenate([np.cos(angle), np.sin(angle)], 2))
    return np.concatenate([high, low, high], 2)


def times_i(x):
    return jnp.concatenate([-x[:, HALF:], x[:, :HALF]], 1)


def packed_fft(values, sign):
    count = len(values)
    if count == 1:
        return values
    even = packed_fft(values[0::2], sign)
    odd = packed_fft(values[1::2], sign)
    half = count // 2
    out = [None] * count
    for k in range(half):
        x = odd[k]
        if k == 0:
            t = x
        elif 4 * k == count:
            t = times_i(x)
            if sign < 0:
                t = -t
        else:
            angle = sign * 2.0 * math.pi * k / count
            t = math.cos(angle) * x + math.sin(angle) * times_i(x)
        out[k] = even[k] + t
        out[k + half] = even[k] - t
    return out


def across(load, store, hold_ref, sign):
    for b in range(4):
        values = packed_fft([load(4 * a + b) for a in range(8)], sign)
        for c in range(8):
            x = values[c]
            if b and c:
                angle = sign * 2.0 * math.pi * b * c / 32
                x = math.cos(angle) * x + math.sin(angle) * times_i(x)
            hold_ref[b, 8 * c : 8 * c + 8, :] = x
    for c in range(8):
        values = packed_fft([hold_ref[b, 8 * c : 8 * c + 8, :] for b in range(4)], sign)
        for d in range(4):
            store(c + 8 * d, values[d])


def split_fft(values, sign):
    count = len(values)
    if count == 1:
        return values
    even = split_fft(values[0::2], sign)
    odd = split_fft(values[1::2], sign)
    half = count // 2
    out = [None] * count
    for k in range(half):
        re, im = odd[k]
        if k == 0:
            t = (re, im)
        elif 4 * k == count:
            t = (-im, re) if sign > 0 else (im, -re)
        else:
            c = math.cos(2.0 * math.pi * k / count)
            s = sign * math.sin(2.0 * math.pi * k / count)
            t = (c * re - s * im, c * im + s * re)
        e = even[k]
        out[k] = (e[0] + t[0], e[1] + t[1])
        out[k + half] = (e[0] - t[0], e[1] - t[1])
    return out


def small_phase(x):
    y = x * x
    c = 1.0 + y * (-1.0 / 2 + y * (1.0 / 24 + y * (-1.0 / 720 + y * (1.0 / 40320 - y / 3628800.0))))
    s = x * (1.0 + y * (-1.0 / 6 + y * (1.0 / 120 + y * (-1.0 / 5040 + y * (1.0 / 362880 - y / 39916800.0)))))
    return c, s


def cmul(x, y):
    return (x[0] * y[0] - x[1] * y[1], x[0] * y[1] + x[1] * y[0])


def block_phases(device, sign):
    shape = (8, HALF)
    step = jnp.full(shape, 1.0, jnp.float32) * (device.astype(jnp.float32) * (sign * 2.0 * math.pi / 256.0))
    one = small_phase(step)
    two = cmul(one, one)
    four = cmul(two, two)
    three = cmul(two, one)
    return [None, one, two, three, four, cmul(four, one), cmul(four, two), cmul(four, three)]


def row_phase(device, start, sign):
    row = (lax.broadcasted_iota(jnp.int32, (8, HALF), 0) + start).astype(jnp.float32)
    scale = sign * 2.0 * math.pi / ORDER
    return small_phase(row * (device * scale if isinstance(device, int) else device.astype(jnp.float32) * scale))


def forward_kernel(x_ref, table_ref, turn_ref, out_ref, part_ref):
    device = lax.axis_index("rows")
    table = table_ref[...]
    for pair in range(RADIX // 2):
        x = jnp.concatenate([x_ref[pl.ds(2 * pair + i, POINTS, stride=RADIX), :] for i in range(2)], 1)
        high = x.astype(jnp.bfloat16)
        low = (x - high.astype(jnp.float32)).astype(jnp.bfloat16)
        part = jnp.dot(table, jnp.concatenate([high, high, low], 0), preferred_element_type=jnp.float32)
        part_ref[2 * pair] = part[:, :HALF]
        part_ref[2 * pair + 1] = part[:, HALF:]
    blocks = block_phases(device, -1.0)
    for g in range(POINTS // 8):
        step = row_phase(32, 8 * g, -1.0)
        turn = row_phase(device, 8 * g, -1.0)
        values = []
        for b in range(RADIX):
            turn = turn if b == 0 else cmul(turn, step)
            part = (part_ref[b, 8 * g : 8 * g + 8, :], part_ref[b, POINTS + 8 * g : POINTS + 8 * g + 8, :])
            values.append(cmul(part, turn))
        values = split_fft(values, -1)
        for k in range(RADIX):
            re, im = values[k] if k == 0 else cmul(values[k], blocks[k])
            at = POINTS * k + 8 * g
            out_ref[at // BAND, at % BAND : at % BAND + 8, :HALF] = re
            out_ref[at // BAND, at % BAND : at % BAND + 8, HALF:] = im


def forward_call(x, turn):
    shape = jax.ShapeDtypeStruct((ROWS, BAND, LANES), jnp.float32)
    table = jnp.asarray(forward_table())
    vmem = pl.BlockSpec(memory_space=pltpu.VMEM)
    return pl.pallas_call(
        forward_kernel,
        out_shape=shape,
        in_specs=[vmem, vmem, pl.BlockSpec(memory_space=pl.ANY)],
        out_specs=vmem,
        scratch_shapes=[pltpu.VMEM((RADIX, 2 * POINTS, HALF), jnp.float32)],
        compiler_params=pltpu.CompilerParams(vmem_limit_bytes=16 * 2**20),
        cost_estimate=pl.CostEstimate(flops=3 * 10**8, bytes_accessed=3 * 2**20, transcendentals=0),
        name="local_forward",
    )(x, table, turn)


def transposed_dot(left, right):
    return lax.dot_general(left, right, (((0,), (0,)), ((), ())), preferred_element_type=jnp.float32)


def coefficient_kernel(block_ref, basis_ref, ordered_ref, coeff_ref, total_ref, scratch_ref, hold_ref):
    for g in range(BAND // 8):

        def load(d):
            return block_ref[d, 8 * g : 8 * g + 8, :]

        def store(j, value):
            scratch_ref[BAND * j + 8 * g : BAND * j + 8 * g + 8, :] = NORM * value

        across(load, store, hold_ref.at[g % 2], -1)
    total = None
    for leaf in range(LEAVES):
        x = scratch_ref[LEAF * leaf : LEAF * (leaf + 1), :]
        rounded = x.astype(jnp.bfloat16)
        turned = times_i(x).astype(jnp.bfloat16)
        ordered_ref[leaf, :LEAF, :] = rounded
        ordered_ref[leaf, LEAF:, :] = turned
        coeff = transposed_dot(basis_ref[leaf, 0], rounded) - transposed_dot(basis_ref[leaf, 1], turned)
        coeff_ref[leaf] = coeff
        total = coeff if total is None else total + coeff
    total_ref[...] = total


def coefficient_call(block, in_basis):
    vmem = pl.BlockSpec(memory_space=pltpu.VMEM)
    return pl.pallas_call(
        coefficient_kernel,
        out_shape=(
            jax.ShapeDtypeStruct((LEAVES, 2 * LEAF, LANES), jnp.bfloat16),
            jax.ShapeDtypeStruct((LEAVES, RANK, LANES), jnp.float32),
            jax.ShapeDtypeStruct((RANK, LANES), jnp.float32),
        ),
        in_specs=[vmem] * 2,
        out_specs=(vmem,) * 3,
        scratch_shapes=[pltpu.VMEM((LENGTH, LANES), jnp.float32), pltpu.VMEM((2, 4, 64, LANES), jnp.float32)],
        compiler_params=pltpu.CompilerParams(vmem_limit_bytes=16 * 2**20),
        cost_estimate=pl.CostEstimate(flops=10**8, bytes_accessed=2 * 2**20, transcendentals=0),
        name="coefficients",
    )(block, in_basis)


def scale_of(level):
    return (2.0 * RANK * LEVELS * 2**level) ** (-0.5)


def with_turned(x):
    return [x.astype(jnp.bfloat16), times_i(x).astype(jnp.bfloat16)]


def stack_couplings(couplings_ref, first, last):
    return jnp.concatenate(
        [
            jnp.concatenate(
                [couplings_ref[leaf, t, part] for t in range(first, last) for part in range(2)], 1
            )
            for leaf in range(LEAVES)
        ],
        0,
    )


def near_kernel(ordered_ref, coeff_ref, blocks_ref, couplings_ref, *refs):
    sibling_refs, own_ref, near_ref = refs[:-2], refs[-2], refs[-1]
    known = len(sibling_refs)
    siblings = []
    for level in range(known):
        siblings += with_turned(scale_of(INNER + level) * sibling_refs[level][...])
    near_ref[...] = jnp.dot(
        stack_couplings(couplings_ref, INNER, INNER + known),
        jnp.concatenate(siblings, 0),
        preferred_element_type=jnp.float32,
    )
    for leaf in range(LEAVES):
        matrix = jnp.concatenate([blocks_ref[leaf, 0], blocks_ref[leaf, 1]], 1)
        own_ref[leaf] = jnp.dot(matrix, ordered_ref[leaf], preferred_element_type=jnp.float32)
        other = 2 * (1 - leaf // 2)
        siblings = with_turned(scale_of(0) * coeff_ref[leaf ^ 1]) + with_turned(
            scale_of(1) * (coeff_ref[other] + coeff_ref[other + 1])
        )
        matrix = jnp.concatenate([couplings_ref[leaf, t, part] for t in range(INNER) for part in range(2)], 1)
        near_ref[RANK * leaf : RANK * (leaf + 1), :] += jnp.dot(
            matrix, jnp.concatenate(siblings, 0), preferred_element_type=jnp.float32
        )


def near_call(ordered, coeff, leaf_blocks, couplings, siblings):
    vmem = pl.BlockSpec(memory_space=pltpu.VMEM)
    return pl.pallas_call(
        near_kernel,
        out_shape=(
            jax.ShapeDtypeStruct((LEAVES, LEAF, LANES), jnp.float32),
            jax.ShapeDtypeStruct((LEAVES * RANK, LANES), jnp.float32),
        ),
        in_specs=[vmem] * (4 + len(siblings)),
        out_specs=(vmem,) * 2,
        compiler_params=pltpu.CompilerParams(vmem_limit_bytes=16 * 2**20),
        cost_estimate=pl.CostEstimate(flops=2 * 10**8, bytes_accessed=4 * 2**20, transcendentals=0),
        name="near_field",
    )(ordered, coeff, leaf_blocks, couplings, *siblings)


def image_kernel(own_ref, near_ref, couplings_ref, basis_ref, *refs):
    sibling_refs, (out_ref, scratch_ref, hold_ref) = refs[:-3], refs[-3:]
    first = LEVELS - len(sibling_refs)
    siblings = []
    for level, ref in enumerate(sibling_refs):
        siblings += with_turned(scale_of(first + level) * ref[...])
    field = near_ref[...] + jnp.dot(
        stack_couplings(couplings_ref, first, LEVELS),
        jnp.concatenate(siblings, 0),
        preferred_element_type=jnp.float32,
    )
    for leaf in range(LEAVES):
        matrix = jnp.concatenate([basis_ref[leaf, 0], basis_ref[leaf, 1]], 1)
        part = jnp.concatenate(with_turned(field[RANK * leaf : RANK * (leaf + 1)]), 0)
        scratch_ref[LEAF * leaf : LEAF * (leaf + 1), :] = own_ref[leaf] + jnp.dot(
            matrix, part, preferred_element_type=jnp.float32
        )
    for g in range(BAND // 8):

        def load(j):
            return scratch_ref[BAND * j + 8 * g : BAND * j + 8 * g + 8, :]

        def store(d, value):
            out_ref[d, 8 * g : 8 * g + 8, :] = value

        across(load, store, hold_ref.at[g % 2], 1)


def image_call(own, near, couplings, out_basis, siblings):
    vmem = pl.BlockSpec(memory_space=pltpu.VMEM)
    return pl.pallas_call(
        image_kernel,
        out_shape=jax.ShapeDtypeStruct((ROWS, BAND, LANES), jnp.float32),
        in_specs=[vmem] * (4 + len(siblings)),
        out_specs=vmem,
        scratch_shapes=[pltpu.VMEM((LENGTH, LANES), jnp.float32), pltpu.VMEM((2, 4, 64, LANES), jnp.float32)],
        compiler_params=pltpu.CompilerParams(vmem_limit_bytes=16 * 2**20),
        cost_estimate=pl.CostEstimate(flops=3 * 10**8, bytes_accessed=4 * 2**20, transcendentals=0),
        name="image",
    )(own, near, couplings, out_basis, *siblings)


def inverse_kernel(block_ref, table_ref, out_ref, turned_ref):
    device = lax.axis_index("rows")
    blocks = block_phases(device, 1.0)
    for g in range(POINTS // 8):
        rows = row_phase(device, 8 * g, 1.0)
        values = []
        for k in range(RADIX):
            phase = rows if k == 0 else cmul(rows, blocks[k])
            at = POINTS * k + 8 * g
            x = block_ref[at // BAND, at % BAND : at % BAND + 8, :]
            values.append(jnp.concatenate(cmul((x[:, :HALF], x[:, HALF:]), phase), 1))
        values = packed_fft(values, 1)
        for b in range(RADIX):
            turned_ref[b, 8 * g : 8 * g + 8, :] = values[b]
    for b in range(RADIX):
        x = turned_ref[b]
        high = x.astype(jnp.bfloat16)
        low = (x - high.astype(jnp.float32)).astype(jnp.bfloat16)
        high_y, low_y = times_i(high), times_i(low)
        value = jnp.dot(
            table_ref[b],
            jnp.concatenate([high, high_y, high, high_y, low, low_y], 0),
            preferred_element_type=jnp.float32,
        )
        out_ref[0, pl.ds(b, POINTS, stride=RADIX), :] = value[:, :HALF]
        out_ref[1, pl.ds(b, POINTS, stride=RADIX), :] = value[:, HALF:]


def inverse_call(block):
    vmem = pl.BlockSpec(memory_space=pltpu.VMEM)
    table = jnp.asarray(inverse_tables())
    return pl.pallas_call(
        inverse_kernel,
        out_shape=jax.ShapeDtypeStruct((2, LENGTH, HALF), jnp.float32),
        in_specs=[vmem] * 2,
        out_specs=vmem,
        scratch_shapes=[pltpu.VMEM((RADIX, POINTS, LANES), jnp.float32)],
        compiler_params=pltpu.CompilerParams(vmem_limit_bytes=16 * 2**20),
        cost_estimate=pl.CostEstimate(flops=3 * 10**8, bytes_accessed=3 * 2**20, transcendentals=0),
        name="local_inverse",
    )(block, table)


def partner(value, mask):
    return lax.ppermute(value, "rows", [(i, i ^ mask) for i in range(ROWS)])


def exchange(total):
    two, one, three = (partner(total, mask) for mask in (2, 1, 3))
    held = total + one + two + three
    siblings = [one, two + three]
    two, one, three = (partner(held, mask) for mask in (8, 4, 12))
    siblings += [one, two + three]
    siblings.append(partner(held + one + two + three, 16))
    return siblings


def second_turn():
    token = jnp.zeros((8, HALF), jnp.float32)
    cores = lax.axis_size("rhs")
    for mask in (8,):
        token = lax.ppermute(
            token,
            ("rows", "rhs"),
            [
                (cores * row + column, cores * (row ^ mask) + column)
                for row in range(ROWS)
                for column in range(0, cores, 2)
            ],
        )
    return token


def swap_blocks(block):
    return lax.all_to_all(block, "rows", split_axis=0, concat_axis=0, tiled=True)


def shards(right_side, leaf_blocks, out_basis, in_basis, couplings):
    block = swap_blocks(forward_call(right_side, second_turn()))
    ordered, coeff, total = coefficient_call(block, in_basis)
    siblings = exchange(total)
    own, near = near_call(ordered, coeff, leaf_blocks, couplings, siblings[:EARLY])
    return inverse_call(swap_blocks(image_call(own, near, couplings, out_basis, siblings[EARLY:])))


def solution(mesh):
    placed = (
        P("rows", "rhs"),
        P("rows", None, None, None),
        P("rows", None, None, None),
        P("rows", None, None, None),
        P("rows", None, None, None, None),
    )
    return jax.shard_map(
        shards, mesh=mesh, in_specs=placed, out_specs=P(None, "rows", "rhs"), check_vma=False
    )
```

```python
import math

import jax
import jax.numpy as jnp
import ml_dtypes
import numpy as np
from jax import lax
from jax.experimental import pallas as pl
from jax.experimental.pallas import tpu as pltpu
from jax.sharding import PartitionSpec as P

HALF = 128
LANES = 2 * HALF
ROWS = 32
BAND = 32
LENGTH = ROWS * BAND
ORDER = LENGTH * ROWS
NORM = 1.0 / math.sqrt(ORDER)
LEAF = 256
RANK = 128
LEVELS = 7
LEAVES = 4
INNER = 2
UPPER = 5
EARLY = 4
RADIX = 8
POINTS = LENGTH // RADIX


def split_table(table):
    high = table.astype(ml_dtypes.bfloat16)
    low = (table - high.astype(np.float64)).astype(ml_dtypes.bfloat16)
    return high, low


def inverse_tables():
    b = np.arange(RADIX)[:, None, None]
    a = np.arange(POINTS)[None, :, None]
    k = np.arange(POINTS)[None, None, :]
    angle = 2.0 * np.pi * (((8 * a + b) * k) % LENGTH) / LENGTH
    high, low = split_table(NORM * np.concatenate([np.cos(angle), np.sin(angle)], 2))
    return np.concatenate([high, low, high], 2)


def times_i(x):
    return jnp.concatenate([-x[:, HALF:], x[:, :HALF]], 1)


def packed_fft(values, sign):
    count = len(values)
    if count == 1:
        return values
    even = packed_fft(values[0::2], sign)
    odd = packed_fft(values[1::2], sign)
    half = count // 2
    out = [None] * count
    for k in range(half):
        x = odd[k]
        if k == 0:
            t = x
        elif 4 * k == count:
            t = times_i(x)
            if sign < 0:
                t = -t
        else:
            angle = sign * 2.0 * math.pi * k / count
            t = math.cos(angle) * x + math.sin(angle) * times_i(x)
        out[k] = even[k] + t
        out[k + half] = even[k] - t
    return out


def across(load, store, hold_ref, sign):
    for b in range(4):
        values = packed_fft([load(4 * a + b) for a in range(8)], sign)
        for c in range(8):
            x = values[c]
            if b and c:
                angle = sign * 2.0 * math.pi * b * c / 32
                x = math.cos(angle) * x + math.sin(angle) * times_i(x)
            hold_ref[b, 8 * c : 8 * c + 8, :] = x
    for c in range(8):
        values = packed_fft([hold_ref[b, 8 * c : 8 * c + 8, :] for b in range(4)], sign)
        for d in range(4):
            store(c + 8 * d, values[d])


def split_fft(values, sign):
    count = len(values)
    if count == 1:
        return values
    even = split_fft(values[0::2], sign)
    odd = split_fft(values[1::2], sign)
    half = count // 2
    out = [None] * count
    for k in range(half):
        re, im = odd[k]
        if k == 0:
            t = (re, im)
        elif 4 * k == count:
            t = (-im, re) if sign > 0 else (im, -re)
        else:
            c = math.cos(2.0 * math.pi * k / count)
            s = sign * math.sin(2.0 * math.pi * k / count)
            t = (c * re - s * im, c * im + s * re)
        e = even[k]
        out[k] = (e[0] + t[0], e[1] + t[1])
        out[k + half] = (e[0] - t[0], e[1] - t[1])
    return out


def small_phase(x):
    y = x * x
    c = 1.0 + y * (-1.0 / 2 + y * (1.0 / 24 + y * (-1.0 / 720 + y * (1.0 / 40320 - y / 3628800.0))))
    s = x * (1.0 + y * (-1.0 / 6 + y * (1.0 / 120 + y * (-1.0 / 5040 + y * (1.0 / 362880 - y / 39916800.0)))))
    return c, s


def cmul(x, y):
    return (x[0] * y[0] - x[1] * y[1], x[0] * y[1] + x[1] * y[0])


def block_phases(device, sign):
    shape = (8, HALF)
    step = jnp.full(shape, 1.0, jnp.float32) * (device.astype(jnp.float32) * (sign * 2.0 * math.pi / 256.0))
    one = small_phase(step)
    two = cmul(one, one)
    four = cmul(two, two)
    three = cmul(two, one)
    return [None, one, two, three, four, cmul(four, one), cmul(four, two), cmul(four, three)]


def row_phase(device, start, sign):
    row = (lax.broadcasted_iota(jnp.int32, (8, HALF), 0) + start).astype(jnp.float32)
    scale = sign * 2.0 * math.pi / ORDER
    return small_phase(row * (device * scale if isinstance(device, int) else device.astype(jnp.float32) * scale))


def forward_table():
    k = lax.broadcasted_iota(jnp.int32, (POINTS, POINTS), 0)
    a = lax.broadcasted_iota(jnp.int32, (POINTS, POINTS), 1)
    turns = jnp.bitwise_and(k * a, POINTS - 1)
    turns = jnp.where(turns < POINTS // 2, turns, turns - POINTS).astype(jnp.float32)
    phase = small_phase(turns * (-2.0 * math.pi / (4 * POINTS)))
    for _ in range(2):
        phase = cmul(phase, phase)
    table = jnp.concatenate(phase, 0)
    high = table.astype(jnp.bfloat16)
    low = (table - high.astype(jnp.float32)).astype(jnp.bfloat16)
    return jnp.concatenate([high, low, high], 1)


def forward_kernel(x_ref, turn_ref, out_ref, part_ref):
    device = lax.axis_index("rows")
    table = forward_table()
    for pair in range(RADIX // 2):
        x = jnp.concatenate([x_ref[pl.ds(2 * pair + i, POINTS, stride=RADIX), :] for i in range(2)], 1)
        high = x.astype(jnp.bfloat16)
        low = (x - high.astype(jnp.float32)).astype(jnp.bfloat16)
        part = jnp.dot(table, jnp.concatenate([high, high, low], 0), preferred_element_type=jnp.float32)
        part_ref[2 * pair] = part[:, :HALF]
        part_ref[2 * pair + 1] = part[:, HALF:]
    blocks = block_phases(device, -1.0)
    for g in range(POINTS // 8):
        step = row_phase(32, 8 * g, -1.0)
        turn = row_phase(device, 8 * g, -1.0)
        values = []
        for b in range(RADIX):
            turn = turn if b == 0 else cmul(turn, step)
            part = (part_ref[b, 8 * g : 8 * g + 8, :], part_ref[b, POINTS + 8 * g : POINTS + 8 * g + 8, :])
            values.append(cmul(part, turn))
        values = split_fft(values, -1)
        for k in range(RADIX):
            re, im = values[k] if k == 0 else cmul(values[k], blocks[k])
            at = POINTS * k + 8 * g
            out_ref[at // BAND, at % BAND : at % BAND + 8, :HALF] = re
            out_ref[at // BAND, at % BAND : at % BAND + 8, HALF:] = im


def forward_call(x, turn):
    shape = jax.ShapeDtypeStruct((ROWS, BAND, LANES), jnp.float32)
    vmem = pl.BlockSpec(memory_space=pltpu.VMEM)
    return pl.pallas_call(
        forward_kernel,
        out_shape=shape,
        in_specs=[vmem, pl.BlockSpec(memory_space=pl.ANY)],
        out_specs=vmem,
        scratch_shapes=[pltpu.VMEM((RADIX, 2 * POINTS, HALF), jnp.float32)],
        compiler_params=pltpu.CompilerParams(vmem_limit_bytes=16 * 2**20),
        cost_estimate=pl.CostEstimate(flops=3 * 10**8, bytes_accessed=3 * 2**20, transcendentals=0),
        name="local_forward",
    )(x, turn)


def transposed_dot(left, right):
    return lax.dot_general(left, right, (((0,), (0,)), ((), ())), preferred_element_type=jnp.float32)


def coefficient_kernel(block_ref, basis_ref, ordered_ref, coeff_ref, total_ref, scratch_ref, hold_ref):
    for g in range(BAND // 8):

        def load(d):
            return block_ref[d, 8 * g : 8 * g + 8, :]

        def store(j, value):
            scratch_ref[BAND * j + 8 * g : BAND * j + 8 * g + 8, :] = NORM * value

        across(load, store, hold_ref.at[g % 2], -1)
    total = None
    for leaf in range(LEAVES):
        x = scratch_ref[LEAF * leaf : LEAF * (leaf + 1), :]
        rounded = x.astype(jnp.bfloat16)
        turned = times_i(x).astype(jnp.bfloat16)
        ordered_ref[leaf, :LEAF, :] = rounded
        ordered_ref[leaf, LEAF:, :] = turned
        coeff = transposed_dot(basis_ref[leaf, 0], rounded) - transposed_dot(basis_ref[leaf, 1], turned)
        coeff_ref[leaf] = coeff
        total = coeff if total is None else total + coeff
    total_ref[...] = total


def coefficient_call(block, in_basis):
    vmem = pl.BlockSpec(memory_space=pltpu.VMEM)
    return pl.pallas_call(
        coefficient_kernel,
        out_shape=(
            jax.ShapeDtypeStruct((LEAVES, 2 * LEAF, LANES), jnp.bfloat16),
            jax.ShapeDtypeStruct((LEAVES, RANK, LANES), jnp.float32),
            jax.ShapeDtypeStruct((RANK, LANES), jnp.float32),
        ),
        in_specs=[vmem] * 2,
        out_specs=(vmem,) * 3,
        scratch_shapes=[pltpu.VMEM((LENGTH, LANES), jnp.float32), pltpu.VMEM((2, 4, 64, LANES), jnp.float32)],
        compiler_params=pltpu.CompilerParams(vmem_limit_bytes=16 * 2**20),
        cost_estimate=pl.CostEstimate(flops=10**8, bytes_accessed=2 * 2**20, transcendentals=0),
        name="coefficients",
    )(block, in_basis)


def scale_of(level):
    return (2.0 * RANK * LEVELS * 2**level) ** (-0.5)


def with_turned(x):
    return [x.astype(jnp.bfloat16), times_i(x).astype(jnp.bfloat16)]


def stack_couplings(couplings_ref, first, last):
    return jnp.concatenate(
        [
            jnp.concatenate(
                [couplings_ref[leaf, t, part] for t in range(first, last) for part in range(2)], 1
            )
            for leaf in range(LEAVES)
        ],
        0,
    )


def near_kernel(ordered_ref, coeff_ref, blocks_ref, couplings_ref, *refs):
    sibling_refs, own_ref, near_ref = refs[:-2], refs[-2], refs[-1]
    known = len(sibling_refs)
    siblings = []
    for level in range(known):
        siblings += with_turned(scale_of(INNER + level) * sibling_refs[level][...])
    near_ref[...] = jnp.dot(
        stack_couplings(couplings_ref, INNER, INNER + known),
        jnp.concatenate(siblings, 0),
        preferred_element_type=jnp.float32,
    )
    for leaf in range(LEAVES):
        matrix = jnp.concatenate([blocks_ref[leaf, 0], blocks_ref[leaf, 1]], 1)
        own_ref[leaf] = jnp.dot(matrix, ordered_ref[leaf], preferred_element_type=jnp.float32)
        other = 2 * (1 - leaf // 2)
        siblings = with_turned(scale_of(0) * coeff_ref[leaf ^ 1]) + with_turned(
            scale_of(1) * (coeff_ref[other] + coeff_ref[other + 1])
        )
        matrix = jnp.concatenate([couplings_ref[leaf, t, part] for t in range(INNER) for part in range(2)], 1)
        near_ref[RANK * leaf : RANK * (leaf + 1), :] += jnp.dot(
            matrix, jnp.concatenate(siblings, 0), preferred_element_type=jnp.float32
        )


def near_call(ordered, coeff, leaf_blocks, couplings, siblings):
    vmem = pl.BlockSpec(memory_space=pltpu.VMEM)
    return pl.pallas_call(
        near_kernel,
        out_shape=(
            jax.ShapeDtypeStruct((LEAVES, LEAF, LANES), jnp.float32),
            jax.ShapeDtypeStruct((LEAVES * RANK, LANES), jnp.float32),
        ),
        in_specs=[vmem] * (4 + len(siblings)),
        out_specs=(vmem,) * 2,
        compiler_params=pltpu.CompilerParams(vmem_limit_bytes=16 * 2**20),
        cost_estimate=pl.CostEstimate(flops=2 * 10**8, bytes_accessed=4 * 2**20, transcendentals=0),
        name="near_field",
    )(ordered, coeff, leaf_blocks, couplings, *siblings)


def image_kernel(own_ref, near_ref, couplings_ref, basis_ref, *refs):
    sibling_refs, (out_ref, scratch_ref, hold_ref) = refs[:-3], refs[-3:]
    first = LEVELS - len(sibling_refs)
    siblings = []
    for level, ref in enumerate(sibling_refs):
        siblings += with_turned(scale_of(first + level) * ref[...])
    field = near_ref[...] + jnp.dot(
        stack_couplings(couplings_ref, first, LEVELS),
        jnp.concatenate(siblings, 0),
        preferred_element_type=jnp.float32,
    )
    for leaf in range(LEAVES):
        matrix = jnp.concatenate([basis_ref[leaf, 0], basis_ref[leaf, 1]], 1)
        part = jnp.concatenate(with_turned(field[RANK * leaf : RANK * (leaf + 1)]), 0)
        scratch_ref[LEAF * leaf : LEAF * (leaf + 1), :] = own_ref[leaf] + jnp.dot(
            matrix, part, preferred_element_type=jnp.float32
        )
    for g in range(BAND // 8):

        def load(j):
            return scratch_ref[BAND * j + 8 * g : BAND * j + 8 * g + 8, :]

        def store(d, value):
            out_ref[d, 8 * g : 8 * g + 8, :] = value

        across(load, store, hold_ref.at[g % 2], 1)


def image_call(own, near, couplings, out_basis, siblings):
    vmem = pl.BlockSpec(memory_space=pltpu.VMEM)
    return pl.pallas_call(
        image_kernel,
        out_shape=jax.ShapeDtypeStruct((ROWS, BAND, LANES), jnp.float32),
        in_specs=[vmem] * (4 + len(siblings)),
        out_specs=vmem,
        scratch_shapes=[pltpu.VMEM((LENGTH, LANES), jnp.float32), pltpu.VMEM((2, 4, 64, LANES), jnp.float32)],
        compiler_params=pltpu.CompilerParams(vmem_limit_bytes=16 * 2**20),
        cost_estimate=pl.CostEstimate(flops=3 * 10**8, bytes_accessed=4 * 2**20, transcendentals=0),
        name="image",
    )(own, near, couplings, out_basis, *siblings)


def inverse_kernel(block_ref, table_ref, out_ref, turned_ref):
    device = lax.axis_index("rows")
    blocks = block_phases(device, 1.0)
    for g in range(POINTS // 8):
        rows = row_phase(device, 8 * g, 1.0)
        values = []
        for k in range(RADIX):
            phase = rows if k == 0 else cmul(rows, blocks[k])
            at = POINTS * k + 8 * g
            x = block_ref[at // BAND, at % BAND : at % BAND + 8, :]
            values.append(jnp.concatenate(cmul((x[:, :HALF], x[:, HALF:]), phase), 1))
        values = packed_fft(values, 1)
        for b in range(RADIX):
            turned_ref[b, 8 * g : 8 * g + 8, :] = values[b]
    for b in range(RADIX):
        x = turned_ref[b]
        high = x.astype(jnp.bfloat16)
        low = (x - high.astype(jnp.float32)).astype(jnp.bfloat16)
        high_y, low_y = times_i(high), times_i(low)
        value = jnp.dot(
            table_ref[b],
            jnp.concatenate([high, high_y, high, high_y, low, low_y], 0),
            preferred_element_type=jnp.float32,
        )
        out_ref[0, pl.ds(b, POINTS, stride=RADIX), :] = value[:, :HALF]
        out_ref[1, pl.ds(b, POINTS, stride=RADIX), :] = value[:, HALF:]


def inverse_call(block):
    vmem = pl.BlockSpec(memory_space=pltpu.VMEM)
    table = jnp.asarray(inverse_tables())
    return pl.pallas_call(
        inverse_kernel,
        out_shape=jax.ShapeDtypeStruct((2, LENGTH, HALF), jnp.float32),
        in_specs=[vmem] * 2,
        out_specs=vmem,
        scratch_shapes=[pltpu.VMEM((RADIX, POINTS, LANES), jnp.float32)],
        compiler_params=pltpu.CompilerParams(vmem_limit_bytes=16 * 2**20),
        cost_estimate=pl.CostEstimate(flops=3 * 10**8, bytes_accessed=3 * 2**20, transcendentals=0),
        name="local_inverse",
    )(block, table)


def partner(value, mask):
    return lax.ppermute(value, "rows", [(i, i ^ mask) for i in range(ROWS)])


def exchange(total):
    two, one, three = (partner(total, mask) for mask in (2, 1, 3))
    held = total + one + two + three
    siblings = [one, two + three]
    two, one, three = (partner(held, mask) for mask in (8, 4, 12))
    siblings += [one, two + three]
    siblings.append(partner(held + one + two + three, 16))
    return siblings


def second_turn():
    token = jnp.zeros((8, HALF), jnp.float32)
    cores = lax.axis_size("rhs")
    for mask in (8,):
        token = lax.ppermute(
            token,
            ("rows", "rhs"),
            [
                (cores * row + column, cores * (row ^ mask) + column)
                for row in range(ROWS)
                for column in range(0, cores, 2)
            ],
        )
    return token


def swap_blocks(block):
    return lax.all_to_all(block, "rows", split_axis=0, concat_axis=0, tiled=True)


def shards(right_side, leaf_blocks, out_basis, in_basis, couplings):
    block = swap_blocks(forward_call(right_side, second_turn()))
    ordered, coeff, total = coefficient_call(block, in_basis)
    siblings = exchange(total)
    own, near = near_call(ordered, coeff, leaf_blocks, couplings, siblings[:EARLY])
    return inverse_call(swap_blocks(image_call(own, near, couplings, out_basis, siblings[EARLY:])))


def solution(mesh):
    placed = (
        P("rows", "rhs"),
        P("rows", None, None, None),
        P("rows", None, None, None),
        P("rows", None, None, None),
        P("rows", None, None, None, None),
    )
    return jax.shard_map(
        shards, mesh=mesh, in_specs=placed, out_specs=P(None, "rows", "rhs"), check_vma=False
    )
```

```python
import math

import jax
import jax.numpy as jnp
import ml_dtypes
import numpy as np
from jax import lax
from jax.experimental import pallas as pl
from jax.experimental.pallas import tpu as pltpu
from jax.sharding import PartitionSpec as P

HALF = 128
LANES = 2 * HALF
ROWS = 32
BAND = 32
LENGTH = ROWS * BAND
ORDER = LENGTH * ROWS
NORM = 1.0 / math.sqrt(ORDER)
LEAF = 256
RANK = 128
LEVELS = 7
LEAVES = 4
INNER = 2
UPPER = 5
PIECES = 2
EARLY = 4
RADIX = 8
POINTS = LENGTH // RADIX


def split_table(table):
    high = table.astype(ml_dtypes.bfloat16)
    low = (table - high.astype(np.float64)).astype(ml_dtypes.bfloat16)
    return high, low


def inverse_tables():
    b = np.arange(RADIX)[:, None, None]
    a = np.arange(POINTS)[None, :, None]
    k = np.arange(POINTS)[None, None, :]
    angle = 2.0 * np.pi * (((8 * a + b) * k) % LENGTH) / LENGTH
    parts = split_table(NORM * np.concatenate([np.cos(angle), np.sin(angle)], 2))
    parts = [part.reshape(RADIX, PIECES, POINTS // PIECES, 2 * POINTS) for part in parts]
    return np.concatenate(parts, 2)


def times_i(x):
    return jnp.concatenate([-x[:, HALF:], x[:, :HALF]], 1)


def packed_fft(values, sign):
    count = len(values)
    if count == 1:
        return values
    even = packed_fft(values[0::2], sign)
    odd = packed_fft(values[1::2], sign)
    half = count // 2
    out = [None] * count
    for k in range(half):
        x = odd[k]
        if k == 0:
            t = x
        elif 4 * k == count:
            t = times_i(x)
            if sign < 0:
                t = -t
        else:
            angle = sign * 2.0 * math.pi * k / count
            t = math.cos(angle) * x + math.sin(angle) * times_i(x)
        out[k] = even[k] + t
        out[k + half] = even[k] - t
    return out


def across(load, store, hold_ref, sign):
    for b in range(4):
        values = packed_fft([load(4 * a + b) for a in range(8)], sign)
        for c in range(8):
            x = values[c]
            if b and c:
                angle = sign * 2.0 * math.pi * b * c / 32
                x = math.cos(angle) * x + math.sin(angle) * times_i(x)
            hold_ref[b, 8 * c : 8 * c + 8, :] = x
    for c in range(8):
        values = packed_fft([hold_ref[b, 8 * c : 8 * c + 8, :] for b in range(4)], sign)
        for d in range(4):
            store(c + 8 * d, values[d])


def split_fft(values, sign):
    count = len(values)
    if count == 1:
        return values
    even = split_fft(values[0::2], sign)
    odd = split_fft(values[1::2], sign)
    half = count // 2
    out = [None] * count
    for k in range(half):
        re, im = odd[k]
        if k == 0:
            t = (re, im)
        elif 4 * k == count:
            t = (-im, re) if sign > 0 else (im, -re)
        else:
            c = math.cos(2.0 * math.pi * k / count)
            s = sign * math.sin(2.0 * math.pi * k / count)
            t = (c * re - s * im, c * im + s * re)
        e = even[k]
        out[k] = (e[0] + t[0], e[1] + t[1])
        out[k + half] = (e[0] - t[0], e[1] - t[1])
    return out


def small_phase(x):
    y = x * x
    c = 1.0 + y * (-1.0 / 2 + y * (1.0 / 24 + y * (-1.0 / 720 + y * (1.0 / 40320 - y / 3628800.0))))
    s = x * (1.0 + y * (-1.0 / 6 + y * (1.0 / 120 + y * (-1.0 / 5040 + y * (1.0 / 362880 - y / 39916800.0)))))
    return c, s


def cmul(x, y):
    return (x[0] * y[0] - x[1] * y[1], x[0] * y[1] + x[1] * y[0])


def block_phases(device, sign):
    shape = (8, HALF)
    step = jnp.full(shape, 1.0, jnp.float32) * (device.astype(jnp.float32) * (sign * 2.0 * math.pi / 256.0))
    one = small_phase(step)
    two = cmul(one, one)
    four = cmul(two, two)
    three = cmul(two, one)
    return [None, one, two, three, four, cmul(four, one), cmul(four, two), cmul(four, three)]


def row_phase(device, start, sign):
    row = (lax.broadcasted_iota(jnp.int32, (8, HALF), 0) + start).astype(jnp.float32)
    scale = sign * 2.0 * math.pi / ORDER
    return small_phase(row * (device * scale if isinstance(device, int) else device.astype(jnp.float32) * scale))


def forward_table():
    k = lax.broadcasted_iota(jnp.int32, (POINTS, POINTS), 0)
    a = lax.broadcasted_iota(jnp.int32, (POINTS, POINTS), 1)
    turns = jnp.bitwise_and(k * a, POINTS - 1)
    turns = jnp.where(turns < POINTS // 2, turns, turns - POINTS).astype(jnp.float32)
    phase = small_phase(turns * (-2.0 * math.pi / (4 * POINTS)))
    for _ in range(2):
        phase = cmul(phase, phase)
    table = jnp.concatenate(phase, 0)
    high = table.astype(jnp.bfloat16)
    low = (table - high.astype(jnp.float32)).astype(jnp.bfloat16)
    return jnp.concatenate([high, low, high], 1)


def forward_kernel(x_ref, turn_ref, out_ref, part_ref):
    device = lax.axis_index("rows")
    table = forward_table()
    for pair in range(RADIX // 2):
        x = jnp.concatenate([x_ref[pl.ds(2 * pair + i, POINTS, stride=RADIX), :] for i in range(2)], 1)
        high = x.astype(jnp.bfloat16)
        low = (x - high.astype(jnp.float32)).astype(jnp.bfloat16)
        part = jnp.dot(table, jnp.concatenate([high, high, low], 0), preferred_element_type=jnp.float32)
        part_ref[2 * pair] = part[:, :HALF]
        part_ref[2 * pair + 1] = part[:, HALF:]
    blocks = block_phases(device, -1.0)
    for g in range(POINTS // 8):
        step = row_phase(32, 8 * g, -1.0)
        turn = row_phase(device, 8 * g, -1.0)
        values = []
        for b in range(RADIX):
            turn = turn if b == 0 else cmul(turn, step)
            part = (part_ref[b, 8 * g : 8 * g + 8, :], part_ref[b, POINTS + 8 * g : POINTS + 8 * g + 8, :])
            values.append(cmul(part, turn))
        values = split_fft(values, -1)
        for k in range(RADIX):
            re, im = values[k] if k == 0 else cmul(values[k], blocks[k])
            at = POINTS * k + 8 * g
            out_ref[at // BAND, at % BAND : at % BAND + 8, :HALF] = re
            out_ref[at // BAND, at % BAND : at % BAND + 8, HALF:] = im


def forward_call(x, turn):
    shape = jax.ShapeDtypeStruct((ROWS, BAND, LANES), jnp.float32)
    vmem = pl.BlockSpec(memory_space=pltpu.VMEM)
    return pl.pallas_call(
        forward_kernel,
        out_shape=shape,
        in_specs=[vmem, pl.BlockSpec(memory_space=pl.ANY)],
        out_specs=vmem,
        scratch_shapes=[pltpu.VMEM((RADIX, 2 * POINTS, HALF), jnp.float32)],
        compiler_params=pltpu.CompilerParams(vmem_limit_bytes=16 * 2**20),
        cost_estimate=pl.CostEstimate(flops=3 * 10**8, bytes_accessed=3 * 2**20, transcendentals=0),
        name="local_forward",
    )(x, turn)


def transposed_dot(left, right):
    return lax.dot_general(left, right, (((0,), (0,)), ((), ())), preferred_element_type=jnp.float32)


def coefficient_kernel(block_ref, basis_ref, ordered_ref, coeff_ref, total_ref, scratch_ref, hold_ref):
    for g in range(BAND // 8):

        def load(d):
            return block_ref[d, 8 * g : 8 * g + 8, :]

        def store(j, value):
            scratch_ref[BAND * j + 8 * g : BAND * j + 8 * g + 8, :] = NORM * value

        across(load, store, hold_ref.at[g % 2], -1)
    total = None
    for leaf in range(LEAVES):
        x = scratch_ref[LEAF * leaf : LEAF * (leaf + 1), :]
        rounded = x.astype(jnp.bfloat16)
        turned = times_i(x).astype(jnp.bfloat16)
        ordered_ref[leaf, :LEAF, :] = rounded
        ordered_ref[leaf, LEAF:, :] = turned
        coeff = transposed_dot(basis_ref[leaf, 0], rounded) - transposed_dot(basis_ref[leaf, 1], turned)
        coeff_ref[leaf] = coeff
        total = coeff if total is None else total + coeff
    total_ref[...] = total


def coefficient_call(block, in_basis):
    vmem = pl.BlockSpec(memory_space=pltpu.VMEM)
    return pl.pallas_call(
        coefficient_kernel,
        out_shape=(
            jax.ShapeDtypeStruct((LEAVES, 2 * LEAF, LANES), jnp.bfloat16),
            jax.ShapeDtypeStruct((LEAVES, RANK, LANES), jnp.float32),
            jax.ShapeDtypeStruct((RANK, LANES), jnp.float32),
        ),
        in_specs=[vmem] * 2,
        out_specs=(vmem,) * 3,
        scratch_shapes=[pltpu.VMEM((LENGTH, LANES), jnp.float32), pltpu.VMEM((2, 4, 64, LANES), jnp.float32)],
        compiler_params=pltpu.CompilerParams(vmem_limit_bytes=16 * 2**20),
        cost_estimate=pl.CostEstimate(flops=10**8, bytes_accessed=2 * 2**20, transcendentals=0),
        name="coefficients",
    )(block, in_basis)


def scale_of(level):
    return (2.0 * RANK * LEVELS * 2**level) ** (-0.5)


def with_turned(x):
    return [x.astype(jnp.bfloat16), times_i(x).astype(jnp.bfloat16)]


def stack_couplings(couplings_ref, first, last):
    return jnp.concatenate(
        [
            jnp.concatenate(
                [couplings_ref[leaf, t, part] for t in range(first, last) for part in range(2)], 1
            )
            for leaf in range(LEAVES)
        ],
        0,
    )


def near_kernel(ordered_ref, coeff_ref, blocks_ref, couplings_ref, *refs):
    sibling_refs, own_ref, near_ref = refs[:-2], refs[-2], refs[-1]
    known = len(sibling_refs)
    siblings = []
    for level in range(known):
        siblings += with_turned(scale_of(INNER + level) * sibling_refs[level][...])
    near_ref[...] = jnp.dot(
        stack_couplings(couplings_ref, INNER, INNER + known),
        jnp.concatenate(siblings, 0),
        preferred_element_type=jnp.float32,
    )
    for leaf in range(LEAVES):
        matrix = jnp.concatenate([blocks_ref[leaf, 0], blocks_ref[leaf, 1]], 1)
        own_ref[leaf] = jnp.dot(matrix, ordered_ref[leaf], preferred_element_type=jnp.float32)
        other = 2 * (1 - leaf // 2)
        siblings = with_turned(scale_of(0) * coeff_ref[leaf ^ 1]) + with_turned(
            scale_of(1) * (coeff_ref[other] + coeff_ref[other + 1])
        )
        matrix = jnp.concatenate([couplings_ref[leaf, t, part] for t in range(INNER) for part in range(2)], 1)
        near_ref[RANK * leaf : RANK * (leaf + 1), :] += jnp.dot(
            matrix, jnp.concatenate(siblings, 0), preferred_element_type=jnp.float32
        )


def near_call(ordered, coeff, leaf_blocks, couplings, siblings):
    vmem = pl.BlockSpec(memory_space=pltpu.VMEM)
    return pl.pallas_call(
        near_kernel,
        out_shape=(
            jax.ShapeDtypeStruct((LEAVES, LEAF, LANES), jnp.float32),
            jax.ShapeDtypeStruct((LEAVES * RANK, LANES), jnp.float32),
        ),
        in_specs=[vmem] * (4 + len(siblings)),
        out_specs=(vmem,) * 2,
        compiler_params=pltpu.CompilerParams(vmem_limit_bytes=16 * 2**20),
        cost_estimate=pl.CostEstimate(flops=2 * 10**8, bytes_accessed=4 * 2**20, transcendentals=0),
        name="near_field",
    )(ordered, coeff, leaf_blocks, couplings, *siblings)


def image_kernel(own_ref, near_ref, couplings_ref, basis_ref, *refs):
    sibling_refs, (out_ref, scratch_ref, hold_ref) = refs[:-3], refs[-3:]
    first = LEVELS - len(sibling_refs)
    siblings = []
    for level, ref in enumerate(sibling_refs):
        siblings += with_turned(scale_of(first + level) * ref[...])
    field = near_ref[...] + jnp.dot(
        stack_couplings(couplings_ref, first, LEVELS),
        jnp.concatenate(siblings, 0),
        preferred_element_type=jnp.float32,
    )
    for leaf in range(LEAVES):
        matrix = jnp.concatenate([basis_ref[leaf, 0], basis_ref[leaf, 1]], 1)
        part = jnp.concatenate(with_turned(field[RANK * leaf : RANK * (leaf + 1)]), 0)
        scratch_ref[LEAF * leaf : LEAF * (leaf + 1), :] = own_ref[leaf] + jnp.dot(
            matrix, part, preferred_element_type=jnp.float32
        )
    for g in range(BAND // 8):

        def load(j):
            return scratch_ref[BAND * j + 8 * g : BAND * j + 8 * g + 8, :]

        def store(d, value):
            out_ref[d, 8 * g : 8 * g + 8, :] = value

        across(load, store, hold_ref.at[g % 2], 1)


def image_call(own, near, couplings, out_basis, siblings):
    vmem = pl.BlockSpec(memory_space=pltpu.VMEM)
    return pl.pallas_call(
        image_kernel,
        out_shape=jax.ShapeDtypeStruct((ROWS, BAND, LANES), jnp.float32),
        in_specs=[vmem] * (4 + len(siblings)),
        out_specs=vmem,
        scratch_shapes=[pltpu.VMEM((LENGTH, LANES), jnp.float32), pltpu.VMEM((2, 4, 64, LANES), jnp.float32)],
        compiler_params=pltpu.CompilerParams(vmem_limit_bytes=16 * 2**20),
        cost_estimate=pl.CostEstimate(flops=3 * 10**8, bytes_accessed=4 * 2**20, transcendentals=0),
        name="image",
    )(own, near, couplings, out_basis, *siblings)


def inverse_kernel(block_ref, table_ref, out_ref, turned_ref, stage_ref, sems):
    device = lax.axis_index("rows")
    blocks = block_phases(device, 1.0)
    for g in range(POINTS // 16):
        halves = []
        for start in (16 * g, 16 * g + 8):
            rows = row_phase(device, start, 1.0)
            values = []
            for k in range(RADIX):
                phase = rows if k == 0 else cmul(rows, blocks[k])
                at = POINTS * k + start
                x = block_ref[at // BAND, at % BAND : at % BAND + 8, :]
                values.append(cmul((x[:, :HALF], x[:, HALF:]), phase))
            halves.append(split_fft(values, 1))
        for b in range(RADIX):
            re, im = (jnp.concatenate([half[b][part] for half in halves], 0) for part in range(2))
            rows = slice(16 * g, 16 * g + 16)
            turned_ref[b, rows, :HALF] = re.astype(jnp.bfloat16)
            turned_ref[b, rows, HALF:] = im.astype(jnp.bfloat16)
            rows = slice(POINTS + 16 * g, POINTS + 16 * g + 16)
            turned_ref[b, rows, :HALF] = (-im).astype(jnp.bfloat16)
            turned_ref[b, rows, HALF:] = re.astype(jnp.bfloat16)
    count = POINTS // PIECES
    copies = []
    for piece in range(PIECES):
        for b in range(RADIX):
            value = jnp.dot(table_ref[b, piece], turned_ref[b], preferred_element_type=jnp.float32)
            value = value[:count] + value[count:]
            for part in range(2):
                rows = pl.ds(RADIX * count * piece + b, count, stride=RADIX)
                stage_ref[part, rows, :] = value[:, HALF * part : HALF * (part + 1)]
        for part in range(2):
            for half in range(2):
                rows = pl.ds(RADIX * count * piece + RADIX * count // 2 * half, RADIX * count // 2)
                copies.append(
                    pltpu.make_async_copy(
                        stage_ref.at[part, rows, :],
                        out_ref.at[part, rows, :],
                        sems.at[4 * piece + 2 * part + half],
                    )
                )
                copies[-1].start()
    for copy in copies:
        copy.wait()


def inverse_call(block):
    vmem = pl.BlockSpec(memory_space=pltpu.VMEM)
    table = jnp.asarray(inverse_tables())
    return pl.pallas_call(
        inverse_kernel,
        out_shape=jax.ShapeDtypeStruct((2, LENGTH, HALF), jnp.float32),
        in_specs=[vmem] * 2,
        out_specs=pl.BlockSpec(memory_space=pltpu.HBM),
        scratch_shapes=[
            pltpu.VMEM((RADIX, 2 * POINTS, LANES), jnp.bfloat16),
            pltpu.VMEM((2, LENGTH, HALF), jnp.float32),
            pltpu.SemaphoreType.DMA((4 * PIECES,)),
        ],
        compiler_params=pltpu.CompilerParams(vmem_limit_bytes=16 * 2**20),
        cost_estimate=pl.CostEstimate(flops=3 * 10**8, bytes_accessed=3 * 2**20, transcendentals=0),
        name="local_inverse",
    )(block, table)


def partner(value, mask):
    return lax.ppermute(value, "rows", [(i, i ^ mask) for i in range(ROWS)])


def exchange(total):
    two, one, three = (partner(total, mask) for mask in (2, 1, 3))
    held = total + one + two + three
    siblings = [one, two + three]
    two, one, three = (partner(held, mask) for mask in (8, 4, 12))
    siblings += [one, two + three]
    siblings.append(partner(held + one + two + three, 16))
    return siblings


def second_turn():
    token = jnp.zeros((8, HALF), jnp.float32)
    cores = lax.axis_size("rhs")
    for mask in (8,):
        token = lax.ppermute(
            token,
            ("rows", "rhs"),
            [
                (cores * row + column, cores * (row ^ mask) + column)
                for row in range(ROWS)
                for column in range(0, cores, 2)
            ],
        )
    return token


def swap_blocks(block):
    return lax.all_to_all(block, "rows", split_axis=0, concat_axis=0, tiled=True)


def shards(right_side, leaf_blocks, out_basis, in_basis, couplings):
    block = swap_blocks(forward_call(right_side, second_turn()))
    ordered, coeff, total = coefficient_call(block, in_basis)
    siblings = exchange(total)
    own, near = near_call(ordered, coeff, leaf_blocks, couplings, siblings[:EARLY])
    return inverse_call(swap_blocks(image_call(own, near, couplings, out_basis, siblings[EARLY:])))


def solution(mesh):
    placed = (
        P("rows", "rhs"),
        P("rows", None, None, None),
        P("rows", None, None, None),
        P("rows", None, None, None),
        P("rows", None, None, None, None),
    )
    return jax.shard_map(
        shards, mesh=mesh, in_specs=placed, out_specs=P(None, "rows", "rhs"), check_vma=False
    )
```
